32 devices in a mesh: dp: 8 (over z, x), mp: 4 (over y, core).
Axes of the slice: x: 2, y: 2, z: 4, core: 2. Of those that a mesh axis runs over, the one named last changes fastest.
Arguments:
- tokens: bfloat16 [8, 8, 96, 768], P(None, 'dp', 'mp'), may hold values from -6 to 6
- w_qkv: bfloat16 [3, 768, 768], P(None, 'mp', 'dp'), may hold values from -0.21875 to 0.21875
- w_out: bfloat16 [768, 768], P('mp', 'dp'), may hold values from -0.625 to 0.625
- w_up: bfloat16 [3072, 768], P('mp', 'dp'), may hold values from -0.21875 to 0.21875
- w_down: bfloat16 [3072, 768], P('mp', 'dp'), may hold values from -0.109375 to 0.109375
- norm_gains: float32 [3, 768], replicated, may hold values from 0.25 to 1.75
- norm_shifts: float32 [3, 768], replicated, may hold values from -1.75 to 1.75
- branch_bias: float32 [2, 768], replicated, may hold values from -1.75 to 1.75
- qv_bias: float32 [2, 768], replicated, may hold values from -1.75 to 1.75
- up_bias: float32 [3072], replicated, may hold values from -1.75 to 1.75
- tl_in: bfloat16 [64, 768], replicated, may hold values from -0.21875 to 0.21875
- tl_bias1: float32 [64], replicated, may hold values from -1.75 to 1.75
- tl_out: bfloat16 [8, 64], replicated, may hold values from -0.75 to 0.75
- tl_bias2: float32 [8], replicated, may hold values from -3 to 3
- keep_mask: int32 [8, 96], replicated, may hold values from 0 to 1, as said below
- assign: int32 [8], replicated, may hold values from 0 to 7, each once
- cotangent: bfloat16 [8, 8, 8, 768], P('dp'), may hold values from -6 to 6
Outputs:
- pooled_out: bfloat16 [8, 8, 8, 768], P('dp')
- grad_tokens: float32 [8, 8, 96, 768], P(None, 'dp', 'mp')
- grad_qkv: float32 [3, 768, 768], P(None, 'mp', 'dp')
- grad_out: float32 [768, 768], P('mp', 'dp')
- grad_up: float32 [3072, 768], P('mp', 'dp')
- grad_down: float32 [3072, 768], P('mp', 'dp')
- grad_gains: float32 [3, 768], replicated
- grad_shifts: float32 [3, 768], replicated
- grad_branch: float32 [2, 768], replicated
- grad_qv: float32 [2, 768], replicated
- grad_upbias: float32 [3072], replicated
- grad_tl_in: float32 [64, 768], replicated
- grad_tl_bias1: float32 [64], replicated
- grad_tl_out: float32 [8, 64], replicated
- grad_tl_bias2: float32 [8], replicated
The draws below stay inside these ranges and needn't reach their ends.
Inputs may be any that keep to these rules, and one draw needn't show every extreme that they name: `keep_mask`: every clip keeps at least one patch. `assign`: each clip appears in exactly one slot.
All inputs are finite; a program needn't handle non-finite values.
Results may differ from the reference program's by a relative error of at most 0.014.
Values may be sent and summed in bfloat16 or wider, within the bound.
No kernel may reach another device: no remote copies, remote signals or barrier semaphores. Data moves between devices by JAX's collectives and lax.ppermute only.
A program may use at most 256 MiB of HBM per device.

```python
import jax
import jax.numpy as jnp
from jax import lax

D = 768
H = 12
HD = 64
FF = 3072
TLH = 64
TLN = 8
P_SIZE = 96
CLIPS = 8
FRAMES = 8


def draw_keep_mask(key, part):
    key = jax.random.fold_in(key, 11)
    first_key, second_key, third_key = jax.random.split(key, 3)
    levels = jax.random.randint(first_key, (CLIPS, P_SIZE), 0, 4)
    cutoff = jax.random.randint(second_key, (CLIPS, 1), 1, 4)
    forced = jax.random.randint(third_key, (CLIPS, 1), 0, P_SIZE)
    places = lax.broadcasted_iota(jnp.int32, (CLIPS, P_SIZE), 1)
    return jnp.where((levels >= cutoff) | (places == forced), 1, 0).astype(jnp.int32)


def shard_levels(rng, shape, cuts, low, largest):
    def one(position, blocks):
        steps = jax.random.uniform(jax.random.fold_in(jax.random.fold_in(rng, 6), position), (blocks,), jnp.float32, low / len(cuts), largest / len(cuts))
        return jnp.repeat(jnp.exp(steps), shape[position] // blocks).reshape((-1,) + (1,) * (len(shape) - position - 1))

    loudness = one(*cuts[0])
    for cut in cuts[1:]:
        loudness = loudness * one(*cut)
    return loudness


def bell_draw(key, dims, scale, bound, cuts=(), dtype=jnp.bfloat16):
    result = scale * jax.random.normal(key, dims, jnp.float32)
    if cuts:
        result = result * shard_levels(key, dims, cuts, -0.22, 0.18)
    return jnp.clip(result, -bound, bound).astype(dtype)


def setup_inputs(seed: int = 0) -> dict:
    key_of = jax.random.split(jax.random.key(seed), 18)
    return {
        "tokens": bell_draw(key_of[0], (CLIPS, FRAMES, P_SIZE, D), 1.0, 6.0, ((1, 8), (2, 4))),
        "w_qkv": bell_draw(key_of[1], (3, D, D), D ** -0.5, 0.21875, ((1, 4), (2, 8))),
        "w_out": bell_draw(key_of[2], (D, D), (D // 8) ** -0.5, 0.625, ((0, 4), (1, 8))),
        "w_up": bell_draw(key_of[3], (FF, D), D ** -0.5, 0.21875, ((0, 4), (1, 8))),
        "w_down": bell_draw(key_of[4], (FF, D), FF ** -0.5, 0.109375, ((0, 4), (1, 8))),
        "norm_gains": jnp.clip(1.0 + 0.15 * jax.random.normal(key_of[5], (3, D), jnp.float32), 0.25, 1.75),
        "norm_shifts": bell_draw(key_of[6], (3, D), 0.3, 1.75, (), jnp.float32),
        "branch_bias": bell_draw(key_of[7], (2, D), 0.3, 1.75, (), jnp.float32),
        "qv_bias": bell_draw(key_of[8], (2, D), 0.3, 1.75, (), jnp.float32),
        "up_bias": bell_draw(key_of[9], (FF,), 0.3, 1.75, (), jnp.float32),
        "tl_in": bell_draw(key_of[10], (TLH, D), D ** -0.5, 0.21875),
        "tl_bias1": bell_draw(key_of[11], (TLH,), 0.3, 1.75, (), jnp.float32),
        "tl_out": bell_draw(key_of[12], (TLN, TLH), TLH ** -0.5, 0.75),
        "tl_bias2": bell_draw(key_of[13], (TLN,), 0.5, 3.0, (), jnp.float32),
        "keep_mask": draw_keep_mask(jax.random.fold_in(key_of[17], 71), 0),
        "assign": jax.random.permutation(key_of[15], CLIPS).astype(jnp.int32),
        "cotangent": bell_draw(key_of[16], (CLIPS, FRAMES, TLN, D), 1.0, 6.0, ((0, 8),)),
    }


eps = 1e-06
HIGH = lax.Precision.HIGHEST

@jax.custom_vjp
def low(v):
    return lax.optimization_barrier(v.astype(jnp.bfloat16)).astype(jnp.float32)

@jax.custom_vjp
def low_back(v):
    return v

def low_keep(v):
    return (low(v), None)

def low_pass(kept, grad):
    return (grad,)

def back_keep(v):
    return (v, None)

def back_low(kept, grad):
    return (low(grad),)
low.defvjp(low_keep, low_pass)
low_back.defvjp(back_keep, back_low)

def layer_norm(values, scale_vec, shift_vec):
    average = lax.optimization_barrier(jnp.mean(values, axis=-1, keepdims=True))
    centered = values - average
    variance = lax.optimization_barrier(jnp.mean(centered * centered, axis=-1, keepdims=True))
    return centered * lax.rsqrt(variance + eps) * scale_vec + shift_vec

def attend(pieces):
    query, key_part, value, keep_row = pieces
    scores = low_back(jnp.einsum('fphe,fqhe->fhpq', query, key_part, precision=HIGH) * HD ** (-0.5))
    scores = jnp.where(keep_row[None, None, None, :] > 0, scores, -1e+30)
    softmaxed = low(jax.nn.softmax(scores, axis=-1))
    return jnp.einsum('fhpq,fqhe->fphe', softmaxed, value, precision=HIGH)

def forward(xf, w_qkv, w_out, w_up, w_down, norm_gains, norm_shifts, branch_bias, qv_bias, up_bias, tl_in, tl_bias1, tl_out, tl_bias2, kept, assign):
    clips_n, frames_n, patches_n = (xf.shape[0], xf.shape[1], xf.shape[2])
    normed_one = low(layer_norm(xf, norm_gains[0], norm_shifts[0]))
    projected = jnp.einsum('cfpi,woi->wcfpo', normed_one, w_qkv, precision=HIGH)
    bias_all = jnp.stack([qv_bias[0], jnp.zeros_like(qv_bias[0]), qv_bias[1]])
    projected = low(low_back(projected + bias_all[:, None, None, None, :]))
    head_view = projected.reshape(3, clips_n, frames_n, patches_n, H, HD)
    attended = lax.map(jax.checkpoint(attend), (head_view[0], head_view[1], head_view[2], kept))
    attended = low(low_back(attended.reshape(clips_n, frames_n, patches_n, D)))
    attn_out = low_back(jnp.einsum('cfpi,io->cfpo', attended, w_out, precision=HIGH))
    residual_one = xf + attn_out + branch_bias[0]
    normed_two = low(layer_norm(residual_one, norm_gains[1], norm_shifts[1]))
    hidden_pre = low_back(jnp.einsum('cfpi,hi->cfph', normed_two, w_up, precision=HIGH) + up_bias)
    hidden_act = low(jax.nn.gelu(hidden_pre, approximate=False))
    mlp_out = low_back(jnp.einsum('cfph,ho->cfpo', hidden_act, w_down, precision=HIGH))
    block_out = residual_one + mlp_out + branch_bias[1]
    tl_input = low(layer_norm(block_out, norm_gains[2], norm_shifts[2]))
    tl_pre = low_back(jnp.einsum('cfpi,ti->cfpt', tl_input, tl_in, precision=HIGH) + tl_bias1)
    tl_hidden = low(jax.nn.gelu(tl_pre, approximate=False))
    map_logits = low_back(jnp.einsum('cfpt,kt->cfpk', tl_hidden, tl_out, precision=HIGH) + tl_bias2)
    map_weight = low(jax.nn.sigmoid(map_logits)) * kept[:, None, :, None]
    kept_count = lax.optimization_barrier(jnp.sum(kept, axis=1))
    pooled = jnp.einsum('cfpk,cfpd->cfkd', map_weight, low(block_out), precision=HIGH) / kept_count[:, None, None, None]
    return pooled[assign]

def reference(tokens, w_qkv, w_out, w_up, w_down, norm_gains, norm_shifts, branch_bias, qv_bias, up_bias, tl_in, tl_bias1, tl_out, tl_bias2, keep_mask, assign, cotangent):
    kept = keep_mask.astype(jnp.float32)
    floats = [item.astype(jnp.float32) for item in (tokens, w_qkv, w_out, w_up, w_down, norm_gains, norm_shifts, branch_bias, qv_bias, up_bias, tl_in, tl_bias1, tl_out, tl_bias2)]

    def forward_all(*params):
        return forward(*params, kept, assign)
    pooled, pullback = jax.vjp(forward_all, *floats)
    grads = pullback(cotangent.astype(jnp.float32))
    return (pooled.astype(jnp.bfloat16), grads[0], grads[1], grads[2], grads[3], grads[4], grads[5], grads[6], grads[7], grads[8], grads[9], grads[10], grads[11], grads[12], grads[13])
```

```python
import functools

import jax
import jax.numpy as jnp
from jax import lax
from jax.experimental import pallas as pl
from jax.experimental.pallas import tpu as pltpu
from jax.sharding import PartitionSpec as P

HD = 64
GROUP = 4
EPS = 1e-06
DOWN = (1, 2, 4)
P1_STEPS = 2
OWN_FIRST = 1
F32 = jnp.float32
BF16 = jnp.bfloat16
COST = {"chip_sum": 4, "ffn_fwd_other": 4, "attn_fwd_own": 4, "pair_second": 0.3, "join": 8, "prep": 0.3, "ffn_fwd_own": 8, "turn": 8, "pair_first": 0.3, "attn_fwd_other": 2, "token_sum": 0.05, "down_grads": 4, "finish": 0.05, "attn_bwd": 16, "attn_grads": 4, "mid_back": 8, "up_grads": 40, "owner_first": 0.3, "turned_sum": 0.3, "learner": 8, "owner_second": 2, "token_bwd": 40, "add_last": 0.3, "early_sum": 0.3, "ffn_bwd_own": 0.05}
ORDER = {"up": (2, 4, 1), "first": (1, 2, 4), "second": (1, 2, 4)}
WAITS = {
    "gate_up": ("wa_n", "own_x",),
    "join_up": ("wa_x0", "wa_z",),
    "gate_down": ("up_n",),
    "attn_fwd_other": ("up_n", "own_x",),
    "attn_fwd_own": ("up_z", "down_n",),
    "chip_sum_0": ("down_n",),
    "join_down": ("wa_x1",),
    "chip_sum_2": ("down_send",),
    "mid_back": ("up_send",),
    "attn_grads": ("down_second",),
    "token_sum": ("first_first", "up_first",),
    "down_second": ("attn_send",),
    "up_first": ("down_first",),
    "up_second": ("attn_send",),
    "token_bwd": ("attn_send",),
    "early_sum": ("first_first",),
    "down_last": ("first_second",),
    "fold": ("first_first",),
    "attn_bwd": ("up_send",),
    "token_last": ("second_second", "first_second",),
    "second_first": ("first_first",),
    "pool_last": ("second_second", "up_second",),
}


def swap(values, axis, bit):
    size = lax.axis_size(axis)
    return lax.ppermute(values, axis, [(i, i ^ bit) for i in range(size)])


def split_axis():
    return lax.axis_size("dp") == 8


def swap_dp(values, bit):
    return swap(values, "dp", bit) if split_axis() else jnp.zeros_like(values)


def dot(left, right):
    return lax.dot_general(left, right, (((1,), (0,)), ((), ())), preferred_element_type=F32)


def dot_nt(left, right):
    return lax.dot_general(left, right, (((1,), (1,)), ((), ())), preferred_element_type=F32)


def dot_tn(left, right):
    return lax.dot_general(left, right, (((0,), (0,)), ((), ())), preferred_element_type=F32)


def gelu_parts(x):
    z = jnp.abs(x) * 0.7071067811865476
    t = 1.0 / (1.0 + 0.3275911 * z)
    bell = jnp.exp(-(z * z))
    series = t * (0.127414796 + t * (-0.142248368 + t * (0.7107068705 + t * (-0.7265760135 + t * 0.5307027145))))
    tail = series * bell
    cdf = jnp.where(x < 0, tail, 1.0 - tail)
    return x * cdf, cdf + x * bell * 0.3989422804014327


def norm_stats(v):
    mean = jnp.mean(v, axis=-1, keepdims=True)
    centered = v - mean
    var = jnp.mean(centered * centered, axis=-1, keepdims=True)
    rstd = lax.rsqrt(var + EPS)
    return centered * rstd, rstd


def norm_back(grad, xhat, rstd, gain):
    scaled = grad * gain
    first = jnp.mean(scaled, axis=-1, keepdims=True)
    second = jnp.mean(scaled * xhat, axis=-1, keepdims=True)
    return (scaled - first - xhat * second) * rstd


def place(parts, order, me_dp, target):
    for part, partners in zip(parts, order):
        rows = part.shape[0] // len(partners)
        for i, j in enumerate(partners):
            if len(order) == 1:
                target[...] = part[...]
            elif j is not None:
                at = pl.ds(pl.multiple_of((me_dp ^ j) * rows, 32), rows)
                target[at, :] = part[i * rows : (i + 1) * rows, :]


def position():
    return lax.axis_index("mp"), lax.axis_index("dp")


def rowsum(v):
    return jnp.sum(v, axis=0, keepdims=True)


def put_halves(target, start, v):
    high = v.astype(BF16)
    rows = v.shape[0]
    target[start : start + rows, :] = high
    target[start + rows : start + 2 * rows, :] = (v - high.astype(F32)).astype(BF16)


def get_halves(source, start, rows):
    return source[start : start + rows, :].astype(F32) + source[start + rows : start + 2 * rows, :].astype(F32)


def head_masks(shape):
    lanes = lax.broadcasted_iota(jnp.int32, shape, 1)
    return [(lanes >= HD * h) & (lanes < HD * (h + 1)) for h in range(shape[1] // HD)]


def stack_heads(v, masks):
    zero = jnp.zeros_like(v)
    return jnp.concatenate([jnp.where(m, v, zero) for m in masks], axis=0)


def merge_heads(stacked, masks):
    rows = masks[0].shape[0]
    out = stacked[0:rows, :]
    for h in range(1, len(masks)):
        out = jnp.where(masks[h], stacked[h * rows : (h + 1) * rows, :], out)
    return out


def join(n, *refs):
    start = 0
    for ref in refs[:n]:
        refs[-1][start : start + ref.shape[0], :] = ref[...]
        start += ref.shape[0]


def turn(first, second, out):
    out[...] = jnp.concatenate([first[...].astype(F32), second[...].astype(F32)], axis=0).T.astype(BF16)


def gate(value, *rest):
    rest[-1][...] = value[...]


def prep(cfg, *refs):
    sc = position()
    G, half, b = cfg
    gains, shifts = refs[4:6]
    x_other, x_own, n_other, n_own, xs = refs[-5:]
    me = sc[0]
    core = me & 1
    for side in (0, 1):
        cside = core if side else 1 - core
        for j in range(4):
            at = pl.ds(pl.multiple_of((cside * half + b * G) * 24, 48), G * 24)
            xs[side * G : (side + 1) * G, me ^ j] = refs[j][at, :].astype(F32).reshape(G, 24, -1)
    gain, shift = gains[0:1, :], shifts[0:1, :]
    for side, x_out, n_out in ((0, x_other, n_other), (1, x_own, n_own)):

        def step(r, carry):
            v = xs[side * G + r].reshape(96, -1)
            at = pl.ds(pl.multiple_of(r * 96, 96), 96)
            x_out[at, :] = v.astype(BF16)
            xhat, _ = norm_stats(v)
            n_out[at, :] = (xhat * gain + shift).astype(BF16)
            return carry

        lax.fori_loop(0, G, step, 0)


def attn_fwd(cfg, *refs):
    sc = position()
    G, half, b, side, order, n_dep = cfg
    n1, keep, bias = refs[0:3]
    n_w = len(order) if order else 1
    w_in = refs[3 : 3 + n_w]
    outs = refs[3 + n_w + n_dep :]
    q_out, k_out, v_out, att, probs, part = outs[:6]
    me, me_dp = sc[0], sc[1]
    core = me & 1
    hcol = att.shape[1]
    heads = hcol // HD
    if order:
        wa = outs[6]
        place(w_in, order, me_dp, wa)
    else:
        wa = w_in[0]
    for w, out in enumerate((q_out, k_out, v_out)):
        t = dot(n1[...], wa[:, w * hcol : (w + 1) * hcol])
        if w != 1:
            row = w // 2
            for m in range(bias.shape[1] // hcol):
                t = t + jnp.where(me == m, bias[row : row + 1, m * hcol : (m + 1) * hcol], 0.0)
        out[...] = t.astype(BF16)
    masks = head_masks((96, hcol))
    clip0 = (core if side else 1 - core) * half + b * G

    def attend(i, carry):
        for r in (2 * i, 2 * i + 1):
            at = pl.ds(pl.multiple_of(r * 96, 96), 96)
            open_row = keep[pl.ds(clip0 + r, 1), :] > 0
            s = dot_nt(stack_heads(q_out[at, :], masks), k_out[at, :]) * HD ** (-0.5)
            s = jnp.where(open_row, s, -1e30)
            e = jnp.exp(s - jnp.max(s, axis=-1, keepdims=True))
            p = (e * (1.0 / jnp.sum(e, axis=-1, keepdims=True))).astype(BF16)
            probs[pl.ds(pl.multiple_of(r * heads * 96, 96), heads * 96), :] = p
            att[at, :] = merge_heads(dot(p, v_out[at, :]), masks).astype(BF16)
        return carry

    lax.fori_loop(0, G // 2, attend, 0, unroll=True)
    part[...] = dot_nt(att[...], wa[:, 3 * hcol : 4 * hcol]).astype(part.dtype)


def chip_sum(part, came, *rest):
    rest[-1][...] = (part[...] + came[...].astype(F32)).astype(BF16)


def mid_norm(mine, came, x, branch, gains, shifts, *rest):
    res, n2 = rest[-2:]
    v = x[...].astype(F32) + (mine[...].astype(F32) + came[...].astype(F32)) + branch[0:1, :]
    res[...] = v
    xhat, _ = norm_stats(v)
    n2[...] = (xhat * gains[1:2, :] + shifts[1:2, :]).astype(BF16)


def ffn_fwd(orders, *refs):
    sc = position()
    n2, bias = refs[0:2]
    if orders:
        n_up, n_w = len(orders[0]), len(orders[0]) + len(orders[1])
        act, slope, part, wu, wd = refs[2 + n_w :]
        place(refs[2 : 2 + n_up], orders[0], sc[1], wu)
        place(refs[2 + n_up : 2 + n_w], orders[1], sc[1], wd)
    else:
        wu, wd, act, slope, part = refs[2:]
    hid = wu.shape[1]
    row_bias = bias[:, pl.ds(pl.multiple_of(sc[0] * hid, 128), hid)]
    tile = 256
    for c in range(hid // tile):
        at = slice(c * tile, (c + 1) * tile)
        pre = dot(n2[...], wu[:, at]) + row_bias[:, at]
        g, d = gelu_parts(pre)
        act[:, at] = g.astype(BF16)
        slope[:, at] = d.astype(BF16)
    part[...] = dot_nt(act[...], wd[...]).astype(part.dtype)


def learner(cfg, assign, *refs):
    sc = position()
    G, half, b, n_cot, ride = cfg
    res, mine, came, branch, gains, shifts, tl_in, tl_b1, tl_out, tl_b2, keep = refs[:11]
    cots = refs[11 : 11 + n_cot]
    grad, grad_low, vec = refs[11 + n_cot : 14 + n_cot]
    R = G * 96
    me_dp = sc[1]
    core = sc[0] & 1
    if n_cot > 1:
        cot = refs[14 + n_cot]
        cot[0:2] = cots[0][0:2]
        cot[2:4] = cots[1][0:2]
        cot[4:8] = cots[2][...]
    else:
        cot = cots[0]
    block = res[...] + (mine[...].astype(F32) + came[...].astype(F32)) + branch[1:2, :]
    low = block.astype(BF16)
    xhat, rstd = norm_stats(block)
    gain = gains[2:3, :]
    tl_x = (xhat * gain + shifts[2:3, :]).astype(BF16)
    pre = dot_nt(tl_x, tl_in[...]) + tl_b1[...]
    hid, slope = gelu_parts(pre)
    hid = hid.astype(BF16)
    logits = dot_nt(hid, tl_out[...]) + tl_b2[...]
    sig = 1.0 / (1.0 + jnp.exp(-logits))
    sig_low = sig.astype(BF16).astype(F32)
    eye = lax.broadcasted_iota(jnp.int32, (96, 96), 0) == lax.broadcasted_iota(jnp.int32, (96, 96), 1)
    pieces, g_maps, pooled = [], [], []
    for g in range(G):
        clip = core * half + b * G + g
        rows = slice(g * 96, (g + 1) * 96)
        keep_row = keep[pl.ds(clip, 1), :].astype(F32)
        inv = 1.0 / jnp.sum(keep_row, axis=1, keepdims=True)
        keep_col = jnp.sum(jnp.where(eye, keep_row, 0.0), axis=1, keepdims=True)
        weight = (sig_low[rows, :] * keep_col).astype(BF16)
        pooled.append(dot_tn(weight, low[rows, :]) * inv)
        at_slot = lax.fori_loop(
            0, assign.shape[0], lambda i, found: jnp.where(assign[i] == clip, i, found), 0, unroll=assign.shape[0] <= 8
        )
        c = cot[at_slot ^ me_dp] if n_cot > 1 else cot[at_slot]
        pieces.append(dot(weight, c) * inv)
        g_maps.append(dot_nt(low[rows, :], c) * inv * keep_col)
    g_map = jnp.concatenate(g_maps, axis=0)
    g_logits = g_map * sig * (1.0 - sig)
    g_low = g_logits.astype(BF16)
    g_hid = dot(g_low, tl_out[...])
    g_pre = (g_hid * slope).astype(BF16)
    g_x = dot(g_pre, tl_in[...])
    total = jnp.concatenate(pieces, axis=0) + norm_back(g_x, xhat, rstd, gain)
    grad[...] = total
    grad_low[0:R, :] = total.astype(BF16)
    grad_low[R : R + 8 * G, :] = jnp.concatenate(pooled, axis=0).astype(BF16)
    hidden = tl_in.shape[0]
    vec[...] = jnp.zeros_like(vec)
    vec[0:hidden, :] = dot_tn(g_pre, tl_x)
    vec[hidden : hidden + 8, 0:hidden] = dot_tn(g_low, hid)
    vec[hidden + 8 : hidden + 9, :] = rowsum(g_x * xhat)
    vec[hidden + 9 : hidden + 10, :] = rowsum(g_x)
    vec[hidden + 10 : hidden + 11, :] = rowsum(total)
    vec[hidden + 11 : hidden + 12, 0:hidden] = rowsum(g_pre.astype(F32))
    vec[hidden + 12 : hidden + 13, 0:8] = rowsum(g_low.astype(F32))
    if ride:
        put_halves(grad_low, R + 8 * G, vec[...])


def ffn_bwd(n_vec, g, slope, wu, wd, *refs):
    part, g_pre, up_sum = refs[n_vec:]
    hid = wu.shape[1]
    R = slope.shape[0]
    tile = 256
    for c in range(hid // tile):
        at = slice(c * tile, (c + 1) * tile)
        v = (dot(g[0:R, :], wd[:, at]) * slope[:, at].astype(F32)).astype(BF16)
        g_pre[:, at] = v
        total = rowsum(v.astype(F32))
        up_sum[:, at] = total + refs[0][:, at] if n_vec else total
    part[...] = dot_nt(g_pre[...], wu[...]).astype(part.dtype)


def partner(order, k):
    return (k >> 1) * order[1] + (k & 1) * order[2]


def weight_grads(cfg, *refs):
    sc = position()
    n_left, n_right, widths, terms_of, cuts, extra, n_extra_in, n_dep = cfg
    lefts, rights = refs[:n_left], refs[n_left : n_left + n_right]
    more = refs[n_left + n_right : n_left + n_right + n_extra_in]
    outs, acc = refs[n_left + n_right + n_extra_in + n_dep : -1], refs[-1]
    n_out = 2 * len(cuts) if cuts else 1
    me_dp = sc[1]
    rows = acc.shape[0]
    tile = 256

    def step(m, carry):
        at = pl.ds(pl.multiple_of(m * tile, tile), tile)
        start = 0
        for width, terms in zip(widths, terms_of):
            total = None
            for left, right in terms:
                n = rights[right].shape[0]
                term = dot_tn(lefts[left][0:n, at], rights[right][...])
                total = term if total is None else total + term
            acc[at, start : start + width] = total
            start += width
        return carry

    lax.fori_loop(0, rows // tile, step, 0, unroll=True)
    if not cuts:
        outs[0][...] = acc[...]
    else:
        size = rows // 8
        start = 0
        for c, (width, order) in enumerate(cuts):
            for k in range(4):
                at = slice(k * size, (k + 1) * size)
                j = partner(order, k)
                far = pl.ds(pl.multiple_of((me_dp ^ j ^ order[0]) * size, 32), size)
                near = pl.ds(pl.multiple_of((me_dp ^ j) * size, 32), size)
                outs[2 * c][at, :] = acc[far, start : start + width].astype(BF16)
                outs[2 * c + 1][at, :] = acc[near, start : start + width]
            start += width
    if extra is not None:
        extra(sc, more, outs[:n_out], outs[n_out:], acc, rights)


def ride_down(half, R, G, sc, more, sent, outs, acc, rights):
    assign, low_own, low_other = more
    me_dp, core = sc[1], sc[0] & 1
    rows = sent[1].shape[0]
    for k in range(4):
        found = []
        for j in (partner(DOWN, k) + DOWN[0], partner(DOWN, k)):
            clip = assign[me_dp ^ j]
            inside = jnp.where(clip < half, clip, clip - half)
            at = pl.ds(pl.multiple_of(R + 8 * inside, 8), 8)
            mine = jnp.where(clip < half, 0, 1) == core
            found.append(jnp.where(mine, low_own[at, :].astype(F32), low_other[at, :].astype(F32)))
        outs[0][8 * k : 8 * k + 8, :] = found[0]
        outs[0][32 + 8 * k : 40 + 8 * k, :] = found[1]
    sent[0][rows : rows + 32, :] = outs[0][0:32, :].astype(BF16)
    quarter = outs[1].shape[0] // 2
    n_vec = 4 * quarter
    total = get_halves(low_own, R + 8 * G, n_vec) + get_halves(low_other, R + 8 * G, n_vec)
    mine = total[0:quarter, :]
    for m in (1, 2, 3):
        mine = jnp.where(sc[0] == m, total[m * quarter : (m + 1) * quarter, :], mine)
    put_halves(outs[1], 0, mine)
    sent[0][rows + 32 : rows + 32 + 2 * quarter, :] = outs[1][...]


def lane_total(v):
    full = v.shape[1] // 128
    total = sum(v[:, 128 * k : 128 * (k + 1)] for k in range(full))
    rest = v.shape[1] - 128 * full
    if rest:
        total = total + jnp.concatenate([v[:, 128 * full :], jnp.zeros((v.shape[0], 128 - rest), F32)], axis=1)
    return rowsum(total.T)


def late_vectors(sc, more, sent, outs, acc, rights):
    wa, gains, shifts, mid_vec, up_sum = more
    vec = outs[-1]
    me = sc[0]
    hcol = wa.shape[1] // 4
    n = len(rights) // 4
    sums = [sum(rowsum(r[...].astype(F32)) for r in rights[w * n : (w + 1) * n]) for w in range(3)]
    row = jnp.concatenate(sums, axis=1)
    vec[...] = jnp.zeros_like(vec)
    vec[0:3, :] = 0.5 * mid_vec[0:3, :]
    for c in range(acc.shape[0] // 256):
        at = slice(256 * c, 256 * (c + 1))
        weight = wa[at, 0 : 3 * hcol].astype(F32)
        shift_grad = lane_total(weight * row)
        vec[3:4, at] = (lane_total(weight * acc[at, 0 : 3 * hcol]) - shifts[0:1, at] * shift_grad) / gains[0:1, at]
        vec[4:5, at] = shift_grad
    vec[pl.ds(5 + me, 1), :] = up_sum[...]
    vec[pl.ds(9 + me, 1), 0:hcol] = sums[0]
    vec[pl.ds(9 + me, 1), 256 : 256 + hcol] = sums[2]
    if len(outs) > 1:
        half = vec.shape[1] // 2
        put_halves(outs[0], 0, jnp.concatenate([vec[:, 0:half], vec[:, half:]], axis=0))
        rows = acc.shape[0] // 2
        sent[0][rows : rows + outs[0].shape[0], :] = outs[0][...]


def mid_back(mine, came, res, grad_block, gains, *rest):
    grad, grad_low, vec = rest[-3:]
    g = mine[...].astype(F32) + came[...].astype(F32)
    xhat, rstd = norm_stats(res[...])
    total = grad_block[...] + norm_back(g, xhat, rstd, gains[1:2, :])
    grad[...] = total
    grad_low[...] = total.astype(BF16)
    vec[...] = jnp.zeros_like(vec)
    vec[0:1, :] = rowsum(g * xhat)
    vec[1:2, :] = rowsum(g)
    vec[2:3, :] = rowsum(total)


def attn_bwd(n_dep, g_own, g_other, *refs):
    own, other = refs[0:4], refs[4:8]
    wa = refs[8]
    outs = refs[9 + n_dep :]
    g_att = outs[6]
    R, hcol = own[0].shape
    heads = hcol // HD
    scale = HD ** (-0.5)
    masks = head_masks((96, hcol))
    for g, (q, k, v, probs), (gq, gk, gv) in ((g_own, own, outs[0:3]), (g_other, other, outs[3:6])):
        g_att[...] = dot(g[...], wa[:, 3 * hcol : 4 * hcol]).astype(BF16)

        def attend(i, carry):
            for r in (2 * i, 2 * i + 1):
                at = pl.ds(pl.multiple_of(r * 96, 96), 96)
                gs = stack_heads(g_att[at, :], masks)
                qs = stack_heads(q[at, :], masks)
                p = probs[pl.ds(pl.multiple_of(r * heads * 96, 96), heads * 96), :]
                pf = p.astype(F32)
                gp = dot_nt(gs, v[at, :])
                inner = jnp.sum(gp * pf, axis=-1, keepdims=True)
                ds = (pf * (gp - inner)).astype(BF16)
                gv[at, :] = dot_tn(p, gs).astype(BF16)
                gq[at, :] = (merge_heads(dot(ds, k[at, :]), masks) * scale).astype(BF16)
                gk[at, :] = (dot_tn(ds, qs) * scale).astype(BF16)
            return carry

        lax.fori_loop(0, R // 192, attend, 0, unroll=True)


def token_bwd(cfg, *refs):
    G, n_dep = cfg
    own, other = refs[0:4], refs[4:8]
    wa, gains, grad_res = refs[8:11]
    near_other, near_own, far, xs, gn_all = refs[11 + n_dep :]
    me = position()[0]
    hcol = own[0].shape[1]
    gain = gains[0:1, :]
    tile = 256
    for side, (gq, gk, gv, x), near in ((1, own, near_own), (0, other, near_other)):

        def spread(c, carry):
            at = pl.ds(pl.multiple_of(c * tile, tile), tile)
            gn_all[:, at] = sum(dot_nt(t[...], wa[at, w * hcol : (w + 1) * hcol]) for w, t in enumerate((gq, gk, gv)))
            return carry

        lax.fori_loop(0, gn_all.shape[1] // tile, spread, 0)

        def back(r, carry):
            at = pl.ds(pl.multiple_of(r * 96, 96), 96)
            gn = gn_all[at, :]
            xhat, rstd = norm_stats(x[at, :].astype(F32))
            gx = norm_back(gn, xhat, rstd, gain)
            if side:
                gx = gx + 0.5 * grad_res[at, :]
            xs[r] = gx.reshape(4, 24, -1)
            return carry

        lax.fori_loop(0, G, back, 0)
        start = 0 if side else 2 * G * 24
        for n in (0, 1):
            near[n * G * 24 : (n + 1) * G * 24, :] = xs[:, me ^ (2 * n)].reshape(G * 24, -1)
            far[start + n * G * 24 : start + (n + 1) * G * 24, :] = (
                xs[:, me ^ (2 * n + 1)].reshape(G * 24, -1).astype(BF16)
            )


def token_sum(near_other, near_own, came, *refs):
    keep, go = refs[-2:]
    core = position()[0] & 1
    size = near_own.shape[0] // 2
    for cside, near, first in ((1 - core, near_other, 0), (core, near_own, 2 * size)):
        at = pl.ds(pl.multiple_of(cside * size, 48), size)
        keep[at, :] = near[0:size, :] + came[first : first + size, :].astype(F32)
        go[at, :] = (near[size:, :] + came[first + size : first + 2 * size, :].astype(F32)).astype(BF16)


def fold(own, came, *refs):
    out = refs[-1]
    n = own.shape[0] - 16
    out[0:n, :] = own[0:n, :].astype(BF16)
    out[n : 2 * n, :] = came[0:n, :].astype(BF16)
    put_halves(out, 2 * n, own[n:, :] + came[n:, :])


def owner_first(ride, came, own, *refs):
    n = own.shape[0] // 2
    if ride:
        kept, early = refs[0:2]
        go, keep, stay, early_out = refs[-4:]
        put_halves(early_out, 0, get_halves(early, 0, early.shape[0] // 2) + get_halves(came, 2 * n + 32, early.shape[0] // 2))
        for k in range(4):
            out, at = (stay, 16 * k) if k < 2 else (go, n + 16 * (k - 2))
            out[at : at + 8, :] = kept[32 + 8 * k : 40 + 8 * k, :].astype(BF16)
            out[at + 8 : at + 16, :] = came[2 * n + 8 * k : 2 * n + 8 * k + 8, :]
        go[n + 32 :, :] = early_out[...]
    else:
        go, keep = refs[-2:]
    go[0:n, :] = (own[n : 2 * n, :] + came[n : 2 * n, :].astype(F32)).astype(BF16)
    keep[...] = own[0:n, :] + came[0:n, :].astype(F32)


def owner_second(ride, came, own, *refs):
    n = own.shape[0] // 2
    if ride:
        stay, early = refs[0:2]
        go, keep, early_out = refs[-3:]
        rows = early.shape[0] // 2
        early_out[...] = (get_halves(early, 0, rows) + get_halves(came, 2 * n + 32, rows)).astype(BF16)
        go[n : n + 16, :] = stay[16:32, :]
        go[n + 16 : n + 32, :] = came[2 * n + 16 : 2 * n + 32, :]
        go[n + 32 :, :] = early_out[...]
    else:
        go, keep = refs[-2:]
    go[0:n, :] = (own[n:, :] + came[n : 2 * n, :].astype(F32)).astype(BF16)
    keep[...] = own[0:n, :] + came[0:n, :].astype(F32)


def late_first(came, own, late, *refs):
    go, keep, late_out = refs[-3:]
    n = own.shape[0] // 2
    rows = late.shape[0] // 2
    put_halves(late_out, 0, get_halves(late, 0, rows) + get_halves(came, 2 * n, rows))
    go[0:n, :] = (own[n : 2 * n, :] + came[n : 2 * n, :].astype(F32)).astype(BF16)
    go[n:, :] = late_out[...]
    keep[...] = own[0:n, :] + came[0:n, :].astype(F32)


def late_second(came, own, late, *refs):
    go, keep, late_out = refs[-3:]
    n = own.shape[0] // 2
    rows = late.shape[0] // 2
    late_out[...] = (get_halves(late, 0, rows) + get_halves(came, 2 * n, rows)).astype(BF16)
    go[0:n, :] = (own[n:, :] + came[n : 2 * n, :].astype(F32)).astype(BF16)
    go[n:, :] = late_out[...]
    keep[...] = own[0:n, :] + came[0:n, :].astype(F32)


def early_sum(own, came, late, late_came, *refs):
    out = refs[-1]
    n = own.shape[0]
    out[0:n, :] = own[...].astype(F32) + came[came.shape[0] - n :, :].astype(F32)
    rows, half = late.shape
    total = late[...].astype(F32) + late_came[late_came.shape[0] - rows :, :].astype(F32)
    out[n:, 0:half] = total[0 : rows // 2, :]
    out[n:, half:] = total[rows // 2 :, :]


def add_last(own, came, *refs):
    out = refs[-1]
    out[...] = own[...] + came[0 : own.shape[0], :].astype(F32)


def turned_sum(n, *refs):
    outs = refs[2 * n :]
    pieces = []
    for i in range(n):
        own, came = refs[2 * i : 2 * i + 2]
        total = own[...] + came[0 : own.shape[0], :].astype(F32)
        pieces.append(total.T)
    at = 0
    flat = pieces[0] if n == 1 else jnp.concatenate(pieces, axis=0)
    for out in outs:
        out[...] = flat[at : at + out.shape[0], :]
        at += out.shape[0]


def cot_first(cot, *refs):
    sc = position()
    far, near = refs[-2:]
    me_dp = sc[1]
    for k in range(4):
        far[k] = cot[me_dp ^ (2 * k + 1)]
        near[k] = cot[me_dp ^ (2 * k)]


def pair_first(near, came, go, stay):
    for i, k in enumerate((1, 3)):
        go[2 * i] = near[k]
        go[2 * i + 1] = came[k]
        stay[2 * i] = near[k - 1]
        stay[2 * i + 1] = came[k - 1]


def pair_second(stay, came, go):
    go[0:2] = stay[2:4]
    go[2:4] = came[2:4]


def pool_last(at, stay, one, two, *refs):
    out = refs[-1]
    me_dp = position()[1]
    for j in range(8):
        rows = (stay[8 * j : 8 * j + 8, :] if j < 2 else one[at[0] + 8 * j - 16 : at[0] + 8 * j - 8, :] if j < 4
                else two[at[1] + 8 * j - 32 : at[1] + 8 * j - 24, :])
        out[me_dp ^ j] = rows


def finish(hcol, n_early, late, came, *refs):
    early = refs[:n_early]
    finish_outs(hcol, late, came, early, *refs[n_early:])


def finish_outs(hcol, late, came, early, gains, shifts, branch, qv, up, tl_in, tl_out, b1, b2, *refs_held):
    if len(early) == 1:
        v = late[...] + came[...]
    else:
        v = get_halves(late, late.shape[0] - 32, 16) + get_halves(came, late.shape[0] - 32, 16)
    hidden = tl_in.shape[0]
    if len(early) == 1:
        total = early[0][...]
    else:
        me, n = position()[0], (early[0].shape[0] - 32) // 2
        held = refs_held[0]
        for i, ref in enumerate(early):
            for k in (0, 1):
                held[pl.ds(pl.multiple_of((me ^ (2 * i + k)) * n, 8), n), :] = ref[k * n : (k + 1) * n, :].astype(F32)
        total = held[...]
    tl_in[...] = total[0:hidden, :]
    tl_out[...] = total[hidden : hidden + 8, 0:hidden]
    rest = total[hidden + 8 : hidden + 16, :]
    b1[...] = rest[3:4, 0:hidden]
    b2[...] = rest[4:5, 0:8]
    gains[...] = jnp.concatenate([v[3:4, :], v[0:1, :], rest[0:1, :]], axis=0)
    shifts[...] = jnp.concatenate([v[4:5, :], v[1:2, :], rest[1:2, :]], axis=0)
    branch[...] = jnp.concatenate([v[2:3, :], rest[2:3, :]], axis=0)
    for m in range(4):
        qv[0:1, m * hcol : (m + 1) * hcol] = v[9 + m : 10 + m, 0:hcol]
        qv[1:2, m * hcol : (m + 1) * hcol] = v[9 + m : 10 + m, 256 : 256 + hcol]
        width = v.shape[1]
        up[0:1, m * width : (m + 1) * width] = v[5 + m : 6 + m, :]


def nbytes(a):
    return a.size * a.dtype.itemsize


def run(kernel, name, outs, ins, smem=0, scratch=(), flops=0, deps=(), smem_more=()):
    spaces = [pltpu.SMEM if i < smem or i in smem_more else pltpu.VMEM for i in range(len(ins) + len(deps))]
    held = sum(nbytes(a) for a in [*ins, *deps, *outs]) + sum(nbytes(s) for s in scratch)
    return pl.pallas_call(
        kernel,
        out_shape=tuple(outs),
        in_specs=[pl.BlockSpec(memory_space=space) for space in spaces],
        out_specs=tuple(pl.BlockSpec(memory_space=pltpu.VMEM) for _ in outs),
        scratch_shapes=[pltpu.VMEM(s.shape, s.dtype) for s in scratch],
        compiler_params=pltpu.CompilerParams(
            vmem_limit_bytes=int(1.25 * held) + 6 * 1024 * 1024 if split_axis() else 56 * 1024 * 1024
        ),
        cost_estimate=pl.CostEstimate(flops=int(1.15e9 * COST.get(name, 1.0)), bytes_accessed=1024, transcendentals=0),
        name=name,
    )(*ins, *deps)


def struct(*shape, dtype=BF16):
    return jax.ShapeDtypeStruct(shape, dtype)


def local(
    tokens, w_qkv, w_out, w_up, w_down, norm_gains, norm_shifts, branch_bias, qv_bias, up_bias,
    tl_in, tl_bias1, tl_out, tl_bias2, keep_mask, assign, cotangent,
):
    clips, frames, patch_dev, D = tokens.shape
    half = clips // 2
    G = GROUP
    n_batch = half // G
    R = G * 96
    hcol = w_qkv.shape[1]
    heads = hcol // HD
    hid = w_up.shape[0]
    tlh = tl_in.shape[0]
    n_mp = lax.axis_size("mp")
    grid = split_axis()
    known = {}

    def waits(name, b=0):
        return [known[item] for item in WAITS.get(name, ()) if item in known] if b == 0 else []

    def gather_dp(values, steps, name=""):
        if not grid:
            return [lax.all_gather(values, "dp", axis=0, tiled=True)], [(0,)], [], []
        if steps == 1:
            along = [swap(values, "dp", 2 * k) for k in (1, 2, 3)]
            across = [swap(item, "dp", 1) for item in [values, *along]]
            return [values, *along, *across], [(0,), (2,), (4,), (6,), (1,), (3,), (5,), (7,)], along, across
        second = swap(values, "dp", 4)
        near = joined([values, second], waits("join_" + name))
        far = swap(near, "dp", 2)
        if steps == 3:
            return [near, far, swap(joined([second, far], waits("rest_" + name)), "dp", 1)], [(0, 4), (2, 6), (5, 3, 7)], None, None
        across = [swap(near, "dp", 1), swap(far, "dp", 1)]
        return [near, far, *across], [(0, 4), (2, 6), (1, 5), (3, 7)], [far], across

    def joined(group, deps=()):
        if len(group) == 1:
            return group[0]
        rows, width = sum(item.shape[0] for item in group), group[0].shape[1]
        out = struct(rows, width, dtype=group[0].dtype)
        return run(functools.partial(join, len(group)), "join", [out], group, deps=deps)[0]

    def after(value, deps):
        return run(gate, "gate", [struct(*value.shape)], [value], deps=deps)[0] if deps else value

    def pair(part, sent, deps=()):
        mine = run(chip_sum, "chip_sum", [struct(R, D)], [part, swap(sent, "mp", 1)], deps=deps)[0]
        return mine, swap(mine, "mp", 2)

    flat = tokens.reshape(clips * patch_dev, D)
    steps = 3 if OWN_FIRST and grid else 2
    if steps == 3:
        across = swap(joined([w_up.T, w_down.T], waits("own")), "dp", 1)
        known.update(own_x=across)
    wa = run(turn, "turn", [struct(w_out.shape[1], 4 * hcol)], [w_qkv.reshape(3 * hcol, -1), w_out])[0]
    far = swap(flat, "mp", 2)
    xs = [flat, swap(flat, "mp", 1), far, swap(far, "mp", 1)]
    wa_parts, wa_order, _, _ = gather_dp(wa, P1_STEPS, "wa")
    known.update(zip(("wa_n", "wa_z", "wa_x0", "wa_x1") if P1_STEPS == 2 else ("wa_n", "wa_z1", "wa_z2", "wa_z3"), wa_parts))
    up_parts, up_order, _, _ = gather_dp(after(w_up.T, waits("gate_up")), steps, "up")
    known.update(zip(("up_n", "up_z", "up_x0", "up_x1"), up_parts))
    down_parts, down_order, _, _ = gather_dp(after(w_down.T, waits("gate_down")), steps, "down")
    known.update(zip(("down_n", "down_z", "down_x0", "down_x1"), down_parts))
    if steps == 3:
        up_parts, up_order = [*up_parts, across], [*up_order, (1, None)]
        down_parts, down_order = [*down_parts, across], [*down_order, (None, 1)]

    if grid:
        blocks = struct(4, 8, D)
        cot_far, cot_near = run(cot_first, "cot_first", [blocks] * 2, [cotangent[0]], deps=waits("cot_first"))
        cot_came = swap(cot_far, "dp", 1)
        cot_go, cot_stay = run(pair_first, "pair_first", [blocks] * 2, [cot_near, cot_came])
        cot_one = swap(cot_go, "dp", 2)
        cot_go = run(pair_second, "pair_second", [blocks], [cot_stay, cot_one])[0]
        cots = [cot_stay, cot_one, swap(cot_go, "dp", 4)]
    else:
        cots = [lax.all_to_all(cotangent, "dp", split_axis=1, concat_axis=0, tiled=True)[:, 0]]
    per_row = 2 * R * D

    early = None
    n_vec = tlh + 64
    kept = []
    wa_all = wf_all = None
    for b in range(n_batch):
        first = b == 0
        x_other, x_own, n_other, n_own = run(
            functools.partial(prep, (G, half, b)), "prep", [struct(R, D)] * 4, [*xs, norm_gains, norm_shifts],
            scratch=[struct(2 * G, 4, 24, D, dtype=F32)], deps=waits("prep", b),
        )

        def attention(side, n1, deps):
            nonlocal wa_all
            fresh = wa_all is None
            weights = wa_parts if fresh else [wa_all]
            outs = [struct(R, hcol)] * 4 + [struct(G * heads * 96, 96), struct(R, D, dtype=F32 if side else BF16)]
            found = run(
                functools.partial(attn_fwd, (G, half, b, side, wa_order if fresh else None, len(deps))),
                "attn_fwd_own" if side else "attn_fwd_other", outs + ([struct(D, 4 * hcol)] if fresh else []),
                [n1, keep_mask, qv_bias, *weights], flops=per_row * 4 * hcol, deps=deps,
            )
            if fresh:
                wa_all = found[6]
            return found[:6]

        a_other = attention(0, n_other, waits("attn_fwd_other", b))
        a_own = attention(1, n_own, waits("attn_fwd_own", b))
        mine, came = pair(a_own[5], a_other[5], waits("chip_sum_0", b))
        res, n2 = run(
            mid_norm, "mid_norm", [struct(R, D, dtype=F32), struct(R, D)],
            [mine, came, x_own, branch_bias, norm_gains, norm_shifts], deps=waits("mid_norm", b),
        )
        n2_other = swap(n2, "mp", 1)

        def ffn(side, rows):
            nonlocal wf_all
            fresh = wf_all is None
            weights = [*up_parts, *down_parts] if fresh else wf_all
            outs = [struct(R, hid)] * 2 + [struct(R, D, dtype=F32 if side else BF16)]
            found = run(
                functools.partial(ffn_fwd, (up_order, down_order) if fresh else None),
                "ffn_fwd_own" if side else "ffn_fwd_other", outs + ([struct(D, hid)] * 2 if fresh else []),
                [rows, up_bias[None, :], *weights], flops=per_row * 2 * hid,
            )
            if fresh:
                wf_all = found[3:]
            return found[:3]

        f_own = ffn(1, n2)
        f_other = ffn(0, n2_other)
        mine, came = pair(f_own[2], f_other[2])
        grad_block, grad_block_low, vec = run(
            functools.partial(learner, (G, half, b, len(cots), grid)), "learner",
            [struct(R, D, dtype=F32), struct(R + 8 * G + (2 * n_vec if grid else 0), D), struct(n_vec, D, dtype=F32)],
            [assign, res, mine, came, branch_bias, norm_gains, norm_shifts, tl_in, tl_bias1[None, :], tl_out,
             tl_bias2[None, :], keep_mask, *cots], smem=1, scratch=[struct(8, 8, D)] if grid else [], flops=per_row * tlh,
        )
        early = vec if first else early + vec
        kept.append((x_other, x_own, n_other, n_own, a_other, a_own, res, n2, n2_other, f_own, f_other, grad_block, grad_block_low))

    def grads(name, groups, widths, cuts, extra=None, more=(), more_outs=(), ride=(), smem_more=(), deps=()):
        lefts, rights, terms = [], [], []
        for pairs in groups:
            mine = []
            for left, right in pairs:
                found = [i for i, known in enumerate(lefts) if known is left]
                if not found:
                    lefts.append(left)
                    found = [len(lefts) - 1]
                rights.append(right)
                mine.append((found[0], len(rights) - 1))
            terms.append(mine)
        width = sum(widths)
        outs = [struct(D, width, dtype=F32)]
        if grid:
            outs = [item for (cut, _), more_rows in zip(cuts, ride or (0,) * len(cuts))
                    for item in (struct(D // 2 + more_rows, cut), struct(D // 2, cut, dtype=F32))]
        base = len(lefts) + len(rights)
        return run(
            functools.partial(weight_grads, (len(lefts), len(rights), widths, terms, cuts if grid else (), extra,
                                             len(more), len(deps))),
            name, outs + list(more_outs), [*lefts, *rights, *more], deps=deps,
            scratch=[struct(D, width, dtype=F32)], flops=n_batch * 2 * per_row * width,
            smem_more=[base + i for i in smem_more],
        )

    def to_owner(order, send, own, rides=(), deps=()):
        size, width = own.shape[0] // 4, own.shape[1]
        ride = 32 + n_vec // 2 if rides else 0
        outs = [struct(2 * size + ride, width), struct(2 * size, width, dtype=F32)]
        outs += [struct(32, width), struct(n_vec // 2, width)] if rides else []
        return run(functools.partial(owner_first, ride), "owner_first", outs, [swap(send, "dp", order[0]), own, *rides], deps=deps)

    def to_last(order, first, deps=()):
        go, own = first[0:2]
        size, width = own.shape[0] // 2, own.shape[1]
        ride = go.shape[0] - 2 * size
        came = swap(go, "dp", order[1])
        outs = [struct(size + (32 + n_vec // 4 if ride else 0), width), struct(size, width, dtype=F32)]
        outs += [struct(n_vec // 4, width)] if ride else []
        go, own, *early = run(functools.partial(owner_second, ride), "owner_second", outs, [came, own, *first[2:]], deps=deps)
        return [own, swap(go, "dp", order[2]), came, *early]

    def turned(sums, heights):
        return run(functools.partial(turned_sum, len(sums)), "turned_sum",
                   [struct(n, sums[0][0].shape[0], dtype=F32) for n in heights], [t for item in sums for t in item[0:2]])

    def last_sum(item, deps=()):
        return run(add_last, "add_last", [struct(*item[0].shape, dtype=F32)], item[0:2], deps=deps)[0].T

    wu, wd = wf_all
    later = []
    sides = range(n_batch)
    halves = []
    for b in sides:
        f_own, f_other, low = kept[b][9], kept[b][10], kept[b][12]
        block_other = swap(low, "mp", 1)
        back_outs = [struct(R, hid), struct(1, hid, dtype=F32)]
        part_own, g_pre_own, up_sum = run(
            functools.partial(ffn_bwd, 0), "ffn_bwd_own", [struct(R, D, dtype=F32)] + back_outs,
            [low, f_own[1], wu, wd], flops=per_row * 2 * hid,
        )
        part_other, g_pre_other, up_sum = run(
            functools.partial(ffn_bwd, 1), "ffn_bwd_other", [struct(R, D)] + back_outs,
            [block_other, f_other[1], wu, wd, up_sum], flops=per_row * 2 * hid,
        )
        halves.append((block_other, g_pre_own, g_pre_other, up_sum, part_own, part_other))

    down_pairs = [p for b in sides for p in ((kept[b][12], kept[b][9][0]), (halves[b][0], kept[b][10][0]))]
    up_pairs = [p for b in sides for p in ((kept[b][7], halves[b][1]), (kept[b][8], halves[b][2]))]
    if grid:
        down_send, down_own, pool_kept, early = grads(
            "down_grads", [down_pairs], (hid,), ((hid, DOWN),), extra=functools.partial(ride_down, half, R, G),
            more=(assign, kept[0][12], halves[0][0]), more_outs=[struct(64, D, dtype=F32), struct(n_vec // 2, D)],
            ride=(32 + n_vec // 2,), smem_more=(0,),
        )
        up_send, up_own = grads("up_grads", [up_pairs], (hid,), ((hid, ORDER["up"]),))
        known.update(down_send=down_send, up_send=up_send)
        down_sums = to_owner(DOWN, down_send, down_own, (pool_kept, early), waits("down_first"))
        known.update(down_first=down_sums[1])
    else:
        down_sums = grads("down_grads", [down_pairs], (hid,), ())
        up_sums = grads("up_grads", [up_pairs], (hid,), ())
        early = lax.psum(early + swap(early, "mp", 1), "dp")

    for b in sides:
        x_other, x_own, n_other, n_own, a_other, a_own, res = kept[b][:7]
        grad_block = kept[b][11]
        block_other, g_pre_own, g_pre_other, up_sum, part_own, part_other = halves[b]
        mine, came = pair(part_own, part_other, waits("chip_sum_2", b))
        grad_res, grad_res_low, mid_vec = run(
            mid_back, "mid_back", [struct(R, D, dtype=F32), struct(R, D), struct(8, D, dtype=F32)],
            [mine, came, res, grad_block, norm_gains], deps=waits("mid_back", b),
        )
        res_other = swap(grad_res_low, "mp", 1)
        deps = waits("attn_bwd", b)
        found = run(
            functools.partial(attn_bwd, len(deps)), "attn_bwd", [struct(R, hcol)] * 6,
            [grad_res_low, res_other, *a_own[:3], a_own[4], *a_other[:3], a_other[4], wa_all],
            scratch=[struct(R, hcol)], deps=deps,
        )
        later.append((res_other, grad_res_low, found[0:3], found[3:6], grad_res, mid_vec, up_sum))
    if grid:
        known.update(late=later[0][2][0])
    mid_total = sum([later[b][5] for b in sides[1:]], later[0][5])
    up_total = sum([later[b][6] for b in sides[1:]], later[0][6])
    *found, late = grads(
        "attn_grads",
        [[p for b in sides for p in ((kept[b][3], later[b][2][w]), (kept[b][2], later[b][3][w]))] for w in range(3)]
        + [[p for b in sides for p in ((later[b][1], kept[b][5][3]), (later[b][0], kept[b][4][3]))]],
        (hcol,) * 4, ((2 * hcol, ORDER["first"]), (2 * hcol, ORDER["second"])), deps=waits("attn_grads"),
        extra=late_vectors, more=(wa_all, norm_gains, norm_shifts, mid_total, up_total), ride=(64, 0) if grid else (),
        more_outs=([struct(64, 2 * hcol)] if grid else []) + [struct(16, D, dtype=F32)],
    )
    if grid:
        known.update(attn_send=found[0])
        halves_first = {}
        size, width = D // 8, 2 * hcol
        for c, name in enumerate(("first", "second")):
            if c:
                halves_first[name] = to_owner(ORDER[name], *found[2 * c : 2 * c + 2], deps=waits(name + "_first"))
            else:
                halves_first[name] = run(
                    late_first, "late_first", [struct(2 * size + 64, width), struct(2 * size, width, dtype=F32), struct(64, width)],
                    [swap(found[0], "dp", ORDER[name][0]), found[1], found[4]], deps=waits(name + "_first"),
                )
            known[name + "_first"] = halves_first[name][1]
        down_z = to_last(DOWN, down_sums, waits("down_second"))
        known.update(down_z2=down_z[1], down_second=down_z[0])
        up_sums = to_owner(ORDER["up"], up_send, up_own, deps=waits("up_first"))
        known.update(up_first=up_sums[1])
        up_z = to_last(ORDER["up"], up_sums, waits("up_second"))
        known.update(up_second=up_z[0], up_z2=up_z[1])
        halves_last = {}
        for name in ("first", "second"):
            if name == "first":
                go, own, late_own = halves_first[name]
                go, own, late_own = run(
                    late_second, "late_second", [struct(size + 32, width), struct(size, width, dtype=F32), struct(32, width)],
                    [swap(go, "dp", ORDER[name][1]), own, late_own], deps=waits("first_second"),
                )
                halves_last[name] = [own, swap(go, "dp", ORDER[name][2]), late_own]
            else:
                halves_last[name] = to_last(ORDER[name], halves_first[name], waits(name + "_second"))
            known[name + "_second"] = halves_last[name][0]

    toks = []
    for b in sides:
        x_other, x_own = kept[b][:2]
        g_own, g_other, grad_res = later[b][2:5]
        rows = 2 * G * 24
        deps = waits("token_bwd", b)
        near_other, near_own, far_both = run(
            functools.partial(token_bwd, (G, len(deps))), "token_bwd", [struct(rows, D, dtype=F32)] * 2 + [struct(2 * rows, D)],
            [*g_own, x_own, *g_other, x_other, wa_all, norm_gains, grad_res],
            scratch=[struct(G, 4, 24, D, dtype=F32), struct(R, D, dtype=F32)], deps=deps,
        )
        tok_own, tok_far = run(
            token_sum, "token_sum", [struct(rows, D, dtype=F32), struct(rows, D)],
            [near_other, near_own, swap(far_both, "mp", 1)], deps=waits("token_sum", b),
        )
        grad_tok = run(add_last, "token_last", [struct(rows, D, dtype=F32)], [tok_own, swap(tok_far, "mp", 2)], deps=waits("token_last", b))[0]
        toks.append(grad_tok.reshape(2, G, 1, patch_dev, D))
    grad_tokens = jnp.stack(toks, axis=1).reshape(clips, 1, patch_dev, D)

    if grid:
        both = run(early_sum, "early_sum", [struct(n_vec // 4 + 16, D, dtype=F32)],
                   [down_z[3], down_z[1], halves_last["first"][2], halves_last["first"][1]], deps=waits("early_sum"))[0]
        late = run(fold, "fold", [struct(n_vec // 2 + 32, D)], [both, swap(both, "mp", 1)], deps=waits("fold"))[0]
        late_came = swap(late, "mp", 2)
        early = [late, late_came]
    else:
        late = late + swap(late, "mp", 1)
        late = lax.psum(late + swap(late, "mp", 2), "dp")
        late_came = jnp.zeros_like(late)
        early = [early]
    gains, shifts, branch, grad_qv, grad_upbias, grad_tl_in, grad_tl_out, grad_b1, grad_b2 = run(
        functools.partial(finish, hcol, len(early)), "finish",
        [struct(3, D, dtype=F32), struct(3, D, dtype=F32), struct(2, D, dtype=F32), struct(2, D, dtype=F32),
         struct(1, n_mp * hid, dtype=F32), struct(tlh, D, dtype=F32), struct(8, tlh, dtype=F32), struct(1, tlh, dtype=F32),
         struct(1, 8, dtype=F32)], [late, late_came, *early],
        scratch=[struct(n_vec, D, dtype=F32)] if grid else [],
    )

    if grid:
        grad_down = last_sum(down_z, waits("down_last"))
        pooled_out = run(functools.partial(pool_last, (D // 4, D // 8)), "pool_last", [struct(8, 8, D)],
                         [down_sums[2], down_z[2], down_z[1]], deps=waits("pool_last"))[0][None]
        grad_up = last_sum(up_z, waits("up_last"))
        grad_qkv, grad_out = turned(
            [halves_last["first"], halves_last["second"]],
            [3 * hcol, hcol],
        )
    else:
        grad_down, grad_up, attn = [
            lax.psum_scatter(item, "dp", scatter_dimension=0, tiled=True).T for item in (down_sums[0], up_sums[0], found[0])
        ]
        grad_qkv, grad_out = attn[: 3 * hcol], attn[3 * hcol :]
        both = jnp.stack([jnp.concatenate([halves[b][0][R:], kept[b][12][R:]], axis=0).reshape(2, G, 8, D) for b in sides], axis=1)
        both = both.reshape(clips, 8, D)
        places = (assign + half * (1 - (lax.axis_index("mp") & 1))) % clips
        table = (places[:, None] == lax.iota(jnp.int32, clips)[None, :]).astype(BF16)
        permuted = jnp.einsum("sc,ckd->skd", table, both, preferred_element_type=F32).astype(BF16)
        pooled_out = lax.all_to_all(permuted[:, None], "dp", split_axis=0, concat_axis=1, tiled=True)
    return (
        pooled_out,
        grad_tokens,
        grad_qkv.reshape(3, hcol, -1),
        grad_out,
        grad_up,
        grad_down,
        gains,
        shifts,
        branch,
        grad_qv,
        grad_upbias[0],
        grad_tl_in,
        grad_b1[0],
        grad_tl_out,
        grad_b2[0],
    )


def solution(mesh):
    in_specs = (
        P(None, "dp", "mp", None),
        P(None, "mp", "dp"),
        P("mp", "dp"),
        P("mp", "dp"),
        P("mp", "dp"),
        P(),
        P(),
        P(),
        P(),
        P(),
        P(),
        P(),
        P(),
        P(),
        P(),
        P(),
        P("dp", None, None, None),
    )
    out_specs = (
        P("dp", None, None, None),
        P(None, "dp", "mp", None),
        P(None, "mp", "dp"),
        P("mp", "dp"),
        P("mp", "dp"),
        P("mp", "dp"),
        P(),
        P(),
        P(),
        P(),
        P(),
        P(),
        P(),
        P(),
        P(),
    )
    return jax.shard_map(local, mesh=mesh, in_specs=in_specs, out_specs=out_specs, check_vma=False)
```
